32 devices in a mesh: dp: 8 (over z, y), tensor: 4 (over x, core).
Axes of the slice: x: 2, y: 2, z: 4, core: 2. Of those that a mesh axis runs over, the one named last changes fastest.
Arguments:
- block_input: bfloat16 [8, 4096, 768], P('dp', 'tensor'), may hold values from -8 to 8
- output_grad: bfloat16 [8, 4096, 768], P('dp', 'tensor'), may hold values from -6 to 6
- segments: int32 [8, 4096], P('dp', 'tensor'), may hold values from 0 to 3, never falling along the last dimension, each value on 1 to 2000 neighbouring positions
- inner_proj: float32 [768, 2, 1536], P('dp', None, 'tensor'), may hold values from -0.21875 to 0.21875
- inner_first: float32 [768, 2, 1536], P('dp', None, 'tensor'), may hold values from -64 to 64
- inner_second: float32 [768, 2, 1536], P('dp', None, 'tensor'), may hold values from 8.192 to 32.768
- step_proj: float32 [768, 24], P('dp', 'tensor'), may hold values from -0.21875 to 0.21875
- step_first: float32 [768, 24], P('dp', 'tensor'), may hold values from -6 to 6
- step_second: float32 [768, 24], P('dp', 'tensor'), may hold values from 0.08192 to 0.32768
- state_proj: float32 [768, 256], P('dp'), may hold values from -0.21875 to 0.21875
- state_first: float32 [768, 256], P('dp'), may hold values from -32 to 32
- state_second: float32 [768, 256], P('dp'), may hold values from 2.94912 to 11.79648
- outer_proj: float32 [768, 1536], P('dp', 'tensor'), may hold values from -0.15625 to 0.15625
- outer_first: float32 [768, 1536], P('dp', 'tensor'), may hold values from -128 to 128
- outer_second: float32 [768, 1536], P('dp', 'tensor'), may hold values from 32.768 to 131.072
- channel_params: float32 [6, 1536], P(None, 'tensor'), may hold values from -0.75 to 2.5
- channel_first: float32 [6, 1536], P(None, 'tensor'), may hold values from -64 to 64
- channel_second: float32 [6, 1536], P(None, 'tensor'), may hold values from 8.192 to 32.768
- head_params: float32 [3, 24], P(None, 'tensor'), may hold values from -6.5 to 2.7
- head_first: float32 [3, 24], P(None, 'tensor'), may hold values from -64 to 64
- head_second: float32 [3, 24], P(None, 'tensor'), may hold values from 8.192 to 32.768
- state_filter: float32 [5, 256], replicated, may hold values from -0.5 to 0.5
- filter_first: float32 [5, 256], replicated, may hold values from -128 to 128
- filter_second: float32 [5, 256], replicated, may hold values from 32.768 to 131.072
- input_gain: float32 [768], replicated, may hold values from 0.5 to 1.5
- gain_first: float32 [768], replicated, may hold values from -80 to 80
- gain_second: float32 [768], replicated, may hold values from 16.384 to 65.536
Outputs:
- block_output: float32 [8, 4096, 768], P('dp', 'tensor')
- input_grad: float32 [8, 4096, 768], P('dp', 'tensor')
- inner_moment: float32 [768, 2, 1536], P('dp', None, 'tensor')
- inner_square: float32 [768, 2, 1536], P('dp', None, 'tensor')
- inner_master: float32 [768, 2, 1536], P('dp', None, 'tensor')
- step_moment: float32 [768, 24], P('dp', 'tensor')
- step_square: float32 [768, 24], P('dp', 'tensor')
- step_master: float32 [768, 24], P('dp', 'tensor')
- state_moment: float32 [768, 256], P('dp')
- state_square: float32 [768, 256], P('dp')
- state_master: float32 [768, 256], P('dp')
- outer_moment: float32 [768, 1536], P('dp', 'tensor')
- outer_square: float32 [768, 1536], P('dp', 'tensor')
- outer_master: float32 [768, 1536], P('dp', 'tensor')
- channel_moment: float32 [6, 1536], P(None, 'tensor')
- channel_square: float32 [6, 1536], P(None, 'tensor')
- channel_master: float32 [6, 1536], P(None, 'tensor')
- head_moment: float32 [3, 24], P(None, 'tensor')
- head_square: float32 [3, 24], P(None, 'tensor')
- head_master: float32 [3, 24], P(None, 'tensor')
- filter_moment: float32 [5, 256], replicated
- filter_square: float32 [5, 256], replicated
- filter_master: float32 [5, 256], replicated
- gain_moment: float32 [768], replicated
- gain_square: float32 [768], replicated
- gain_master: float32 [768], replicated
The draws below stay inside these ranges and needn't reach their ends.
Inputs may be any that keep to these rules, and one draw needn't show every extreme that they name: `segments`: segment numbers never fall along a sequence; each sequence holds 4 documents, each of 1 to 2000 tokens, one of exactly 2000.
All inputs are finite; a program needn't handle non-finite values.
Results may differ from the reference program's by a relative error of at most 0.006.
The reference program's roundings to bfloat16 on the way count: a program that leaves them out, or rounds other values in their place, can miss the bound.
Values may be sent and summed in bfloat16 or wider, within the bound.
A program may use at most 192 MiB of HBM per device.

```python
import math
from functools import partial
import jax
import jax.numpy as jnp
import numpy as np
from jax import lax

D_MODEL = 768
D_INNER = 1536
HEADS = 24
HEAD_DIM = 64
D_STATE = 128
CONV = 4
SPAN = 256
LENGTH = 4096
DOCS = 4
DOC_MOST = 2000
STEP = 10
SEQUENCES = 8
TOKENS = 32768


def draw_channel_params(key, part):
    key = jax.random.fold_in(key, 21)
    key_taps, key_bias, key_gain = jax.random.split(key, 3)
    placed = jnp.arange(D_INNER, dtype=jnp.float32) / (D_INNER - 1)
    taps_part = jax.random.uniform(key_taps, (CONV, D_INNER), jnp.float32, -0.5, 0.5) * (0.7 + 0.8 * placed)
    bias_part = jax.random.uniform(key_bias, (1, D_INNER), jnp.float32, -0.3, 0.3)
    gain_part = (0.6 + 1.2 * placed) * jnp.clip(1.0 + 0.08 * jax.random.normal(key_gain, (D_INNER,), jnp.float32), 0.75, 1.25)
    return jnp.concatenate([taps_part, bias_part, gain_part[None, :]], 0)


def draw_head_params(key, part):
    key = jax.random.fold_in(key, 22)
    key_bias, key_rate, key_skip = jax.random.split(key, 3)
    placed = jnp.arange(HEADS, dtype=jnp.float32) / (HEADS - 1)
    step_bias = jax.random.uniform(key_bias, (HEADS,), jnp.float32, -6.5, -2.5)
    log_rate = jax.random.uniform(key_rate, (HEADS,), jnp.float32, 0.0, 2.7)
    skip_part = (0.5 + placed) * jax.random.uniform(key_skip, (HEADS,), jnp.float32, 0.85, 1.15)
    return jnp.stack([step_bias, log_rate, skip_part], 0)


def with_spikes(values, own_key, source, target, blocks, factor):
    owner, partner = [(jnp.arange(values.shape[dim]) // (values.shape[dim] // blocks)).reshape([-1 if axis == dim else 1 for axis in range(values.ndim)]) for dim in (source, target)]
    chosen = jax.random.permutation(own_key, blocks)[partner]
    strong = (owner == chosen) | (owner == (partner + blocks // 2) % blocks)
    return jnp.where(strong, factor * values, values)


def shard_levels(rng, extent, cuts, low, top_value):
    def one(dim, blocks):
        draws = jax.random.uniform(jax.random.fold_in(jax.random.fold_in(rng, 6), dim), (blocks,), jnp.float32, low / len(cuts), top_value / len(cuts))
        return jnp.repeat(jnp.exp(draws), extent[dim] // blocks).reshape((-1,) + (1,) * (len(extent) - dim - 1))

    gain = one(*cuts[0])
    for cut in cuts[1:]:
        gain = gain * one(*cut)
    return gain


def profile(count, total, reach, skew):
    weights = [(1 << 20) // math.isqrt(standing ** skew) + 1 for standing in range(2, count + 1)]
    rest, holding = total - reach - (count - 1), [1] * (count - 1)
    while rest > 0:
        candidates = [i for i in range(count - 1) if holding[i] < reach]
        whole, remaining = sum([weights[i] for i in candidates]), rest
        for i in candidates:
            extra = min(reach - holding[i], max(1, remaining * weights[i] // whole), rest)
            holding[i] = holding[i] + extra
            rest = rest - extra
    return np.array([reach] + holding)


def ragged_sizes(rng, number_of, total, limit, slope):
    if number_of == 2:
        one = jax.random.randint(rng, (), max(1, total - limit), min(limit, total - 1) + 1)
        return jnp.stack([one, total - one])
    sizes = jnp.asarray(profile(number_of, total, limit, slope), jnp.int32)
    couples = (number_of - 1) // 2
    donor, taker = sizes[1:1 + 2 * couples:2], sizes[2:2 + 2 * couples:2]
    slack = jnp.minimum(donor - 1, limit - taker)
    moved = jax.random.randint(jax.random.fold_in(rng, 1), (couples,), 0, 1 << 20) % (slack + 1)
    sizes = sizes.at[1:1 + 2 * couples:2].set(donor - moved).at[2:2 + 2 * couples:2].set(taker + moved)
    return sizes[jax.random.permutation(jax.random.fold_in(rng, 2), number_of)]


def bell_draw(own_key, extent, deviation, reach, cuts=(), kind=jnp.bfloat16):
    factor_of = shard_levels(own_key, extent, cuts, -0.22, 0.18) if cuts else 1.0
    entries = jax.random.normal(own_key, extent, jnp.float32) * deviation * factor_of
    return jnp.minimum(jnp.maximum(entries, -reach), reach).astype(kind)


def gaussian_with(stream_key, extent, scale, bound, cuts, heavy, kind=jnp.bfloat16):
    values = scale * jax.random.normal(stream_key, extent, jnp.float32)
    if cuts:
        values = values * shard_levels(stream_key, extent, cuts, -0.22, 0.18)
    return jnp.clip(with_spikes(values, jax.random.fold_in(stream_key, 3), *heavy), -bound, bound).astype(kind)


def setup_inputs(seed: int = 0) -> dict:
    key_list = jax.random.split(jax.random.key(seed), 28)
    return {
        "block_input": gaussian_with(key_list[0], (SEQUENCES, LENGTH, D_MODEL), 1.0, 8.0, ((0, 8), (1, 4)), (0, 2, 8, 2.0)),
        "output_grad": bell_draw(key_list[1], (SEQUENCES, LENGTH, D_MODEL), 1.0, 6.0, ((0, 8), (1, 4))),
        "segments": jax.vmap(lambda own: jnp.searchsorted(jnp.cumsum(ragged_sizes(own, DOCS, LENGTH, DOC_MOST, 2)), jnp.arange(LENGTH), side="right"))(jax.random.split(key_list[2], SEQUENCES)).reshape((SEQUENCES, LENGTH)).astype(jnp.int32),
        "inner_proj": bell_draw(key_list[3], (D_MODEL, 2, D_INNER), D_MODEL ** -0.5, 0.21875, ((0, 8), (2, 4)), jnp.float32),
        "inner_first": bell_draw(key_list[4], (D_MODEL, 2, D_INNER), (0.055 * TOKENS ** 0.5), 64.0, ((0, 8), (2, 4)), jnp.float32),
        "inner_second": jnp.clip(jnp.exp(math.log(32.768) - 1.3862944 * jax.random.uniform(key_list[5], (D_MODEL, 2, D_INNER), jnp.float32) ** shard_levels(key_list[5], (D_MODEL, 2, D_INNER), ((0, 8), (2, 4)), -0.2, 0.2)), 8.192, 32.768),
        "step_proj": bell_draw(key_list[6], (D_MODEL, HEADS), D_MODEL ** -0.5, 0.21875, ((0, 8), (1, 4)), jnp.float32),
        "step_first": bell_draw(key_list[7], (D_MODEL, HEADS), (0.0055 * TOKENS ** 0.5), 6.0, ((0, 8), (1, 4)), jnp.float32),
        "step_second": jnp.clip(jnp.exp(math.log(0.32768) - 1.3862944 * jax.random.uniform(key_list[8], (D_MODEL, HEADS), jnp.float32) ** shard_levels(key_list[8], (D_MODEL, HEADS), ((0, 8), (1, 4)), -0.2, 0.2)), 0.08192, 0.32768),
        "state_proj": bell_draw(key_list[9], (D_MODEL, 2 * D_STATE), D_MODEL ** -0.5, 0.21875, ((0, 8),), jnp.float32),
        "state_first": bell_draw(key_list[10], (D_MODEL, 2 * D_STATE), (0.033 * TOKENS ** 0.5), 32.0, ((0, 8),), jnp.float32),
        "state_second": jnp.clip(jnp.exp(math.log(11.79648) - 1.3862944 * jax.random.uniform(key_list[11], (D_MODEL, 2 * D_STATE), jnp.float32) ** shard_levels(key_list[11], (D_MODEL, 2 * D_STATE), ((0, 8),), -0.2, 0.2)), 2.94912, 11.79648),
        "outer_proj": bell_draw(key_list[12], (D_MODEL, D_INNER), D_INNER ** -0.5, 0.15625, ((0, 8), (1, 4)), jnp.float32),
        "outer_first": bell_draw(key_list[13], (D_MODEL, D_INNER), (0.111 * TOKENS ** 0.5), 128.0, ((0, 8), (1, 4)), jnp.float32),
        "outer_second": jnp.clip(jnp.exp(math.log(131.072) - 1.3862944 * jax.random.uniform(key_list[14], (D_MODEL, D_INNER), jnp.float32) ** shard_levels(key_list[14], (D_MODEL, D_INNER), ((0, 8), (1, 4)), -0.2, 0.2)), 32.768, 131.072),
        "channel_params": draw_channel_params(jax.random.fold_in(key_list[27], 71), 0),
        "channel_first": bell_draw(key_list[16], (CONV + 2, D_INNER), (0.055 * TOKENS ** 0.5), 64.0, ((1, 4),), jnp.float32),
        "channel_second": jnp.clip(jnp.exp(math.log(32.768) - 1.3862944 * jax.random.uniform(key_list[17], (CONV + 2, D_INNER), jnp.float32) ** shard_levels(key_list[17], (CONV + 2, D_INNER), ((1, 4),), -0.2, 0.2)), 8.192, 32.768),
        "head_params": draw_head_params(jax.random.fold_in(key_list[27], 71), 0),
        "head_first": bell_draw(key_list[19], (3, HEADS), (0.055 * TOKENS ** 0.5), 64.0, ((1, 4),), jnp.float32),
        "head_second": jnp.clip(jnp.exp(math.log(32.768) - 1.3862944 * jax.random.uniform(key_list[20], (3, HEADS), jnp.float32) ** shard_levels(key_list[20], (3, HEADS), ((1, 4),), -0.2, 0.2)), 8.192, 32.768),
        "state_filter": jnp.clip(jax.random.uniform(key_list[21], (CONV + 1, 2 * D_STATE), jnp.float32, -0.5, 0.5), -0.5, 0.5),
        "filter_first": bell_draw(key_list[22], (CONV + 1, 2 * D_STATE), (0.111 * TOKENS ** 0.5), 128.0, (), jnp.float32),
        "filter_second": jnp.clip(jnp.exp(jax.random.uniform(key_list[23], (CONV + 1, 2 * D_STATE), jnp.float32, math.log(32.768), math.log(131.072))), 32.768, 131.072),
        "input_gain": jnp.clip(1.0 + 0.1 * jax.random.normal(key_list[24], (D_MODEL,), jnp.float32), 0.5, 1.5),
        "gain_first": bell_draw(key_list[25], (D_MODEL,), (0.078 * TOKENS ** 0.5), 80.0, (), jnp.float32),
        "gain_second": jnp.clip(jnp.exp(jax.random.uniform(key_list[26], (D_MODEL,), jnp.float32, math.log(16.384), math.log(65.536))), 16.384, 65.536),
    }


NORM_EPS = 1e-05
BETA_ONE = 0.9
BETA_TWO = 0.999
ADAM_EPS = 1e-08
MATRIX_RATE = 0.1
VECTOR_RATE = 0.3
MATRIX_DECAY = 0.1
HIGHEST = lax.Precision.HIGHEST

@jax.custom_vjp
def low(v):
    return lax.optimization_barrier(v.astype(jnp.bfloat16)).astype(jnp.float32)

@jax.custom_vjp
def low_back(v):
    return v

def low_keep(v):
    return (low(v), None)

def low_pass(kept, grad):
    return (grad,)

def back_keep(v):
    return (v, None)

def back_low(kept, grad):
    return (low(grad),)
low.defvjp(low_keep, low_pass)
low_back.defvjp(back_keep, back_low)

def causal_filter(values, filter_taps, filter_bias, segment):
    taps_count = filter_taps.shape[0]
    seq_len = values.shape[-2]
    filtered = filter_bias + filter_taps[taps_count - 1] * values
    for offset in range(1, taps_count):
        leading = [(0, 0)] * (values.ndim - 2)
        shifted = jnp.pad(values, leading + [(offset, 0), (0, 0)])[..., :seq_len, :]
        earlier = jnp.pad(segment, leading + [(offset, 0)], constant_values=-1)[..., :seq_len]
        same_doc = (earlier == segment).astype(values.dtype)
        filtered = filtered + filter_taps[taps_count - 1 - offset] * shifted * same_doc[..., None]
    return filtered

def span_step(rates, skip, carry, pieces):
    carry_state, last_seg = carry
    block_x, block_b, block_c, block_dt, block_seg = pieces
    block_rows = block_seg.shape[0]
    log_decay = jnp.cumsum(block_dt * rates, axis=0)
    positions = jnp.arange(block_rows)
    same_doc = (block_seg[:, None] == block_seg[None, :]) & (positions[:, None] >= positions[None, :])
    log_gaps = log_decay.T[:, :, None] - log_decay.T[:, None, :]
    decays = jnp.where(same_doc[None], jnp.exp(jnp.where(same_doc[None], log_gaps, 0.0)), 0.0)
    scores = jnp.dot(block_c, block_b.T, precision=HIGHEST)
    weights = decays * scores[None] * block_dt.T[:, None, :]
    inner_part = jnp.einsum('hts,shp->thp', weights, block_x, precision=HIGHEST)
    carried = jnp.where((block_seg == last_seg)[:, None], jnp.exp(log_decay), 0.0)
    outer_part = jnp.einsum('hpn,tn->thp', carry_state, block_c, precision=HIGHEST) * carried[:, :, None]
    end_seg = block_seg[block_rows - 1]
    tail_weight = jnp.where((block_seg == end_seg)[:, None], jnp.exp(log_decay[block_rows - 1][None, :] - log_decay), 0.0) * block_dt
    kept = jnp.where(last_seg == end_seg, jnp.exp(log_decay[block_rows - 1]), 0.0)
    fresh_state = jnp.einsum('th,thp,tn->hpn', tail_weight, block_x, block_b, precision=HIGHEST)
    new_state = carry_state * kept[:, None, None] + fresh_state
    result = inner_part + outer_part + skip[None, :, None] * block_x
    return ((new_state, end_seg), result)

def scan_states(inputs_x, inputs_b, inputs_c, step_sizes, segment, rates, skip):
    seq_len = inputs_x.shape[0]
    blocks = seq_len // SPAN

    def split_blocks(values):
        return values.reshape((blocks, SPAN) + values.shape[1:])
    start = (jnp.zeros((inputs_x.shape[1], inputs_x.shape[2], inputs_b.shape[1]), jnp.float32), jnp.array(-1, jnp.int32))
    step_fn = jax.checkpoint(partial(span_step, rates, skip))
    final, outputs = lax.scan(step_fn, start, (split_blocks(inputs_x), split_blocks(inputs_b), split_blocks(inputs_c), split_blocks(step_sizes), split_blocks(segment)))
    return outputs.reshape(inputs_x.shape)

def adam_update(weight, gradient, moment_one, moment_two, step_rate, decay_rate):
    first_new = BETA_ONE * moment_one + (1.0 - BETA_ONE) * gradient
    second_new = BETA_TWO * moment_two + (1.0 - BETA_TWO) * gradient * gradient
    first_hat = first_new / (1.0 - BETA_ONE ** STEP)
    second_hat = second_new / (1.0 - BETA_TWO ** STEP)
    weight_new = weight - step_rate * (first_hat / (jnp.sqrt(second_hat) + ADAM_EPS) + decay_rate * weight)
    return (first_new, second_new, weight_new)

def reference(block_input, output_grad, segments, inner_proj, inner_first, inner_second, step_proj, step_first, step_second, state_proj, state_first, state_second, outer_proj, outer_first, outer_second, channel_params, channel_first, channel_second, head_params, head_first, head_second, state_filter, filter_first, filter_second, input_gain, gain_first, gain_second):
    stream = block_input.astype(jnp.float32)
    cotangent = output_grad.astype(jnp.float32)

    def forward(stream, inner_proj, step_proj, state_proj, outer_proj, channel_params, head_params, state_filter, input_gain):
        inner_weight = low(inner_proj).reshape(D_MODEL, 2 * D_INNER)
        step_weight = low(step_proj)
        state_weight = low(state_proj)
        outer_weight = low(outer_proj)

        def one_sequence(pieces):
            seq_rows, segment = pieces
            row_scale = lax.rsqrt(lax.optimization_barrier(jnp.mean(seq_rows * seq_rows, -1, keepdims=True)) + NORM_EPS)
            normed = low(seq_rows * row_scale * input_gain)
            mixed_cols = low_back(jnp.dot(normed, inner_weight, precision=HIGHEST, preferred_element_type=jnp.float32))
            gate_raw = mixed_cols[:, :D_INNER]
            inner_raw = mixed_cols[:, D_INNER:]
            step_raw = low_back(jnp.dot(normed, step_weight, precision=HIGHEST, preferred_element_type=jnp.float32))
            state_raw = low_back(jnp.dot(normed, state_weight, precision=HIGHEST, preferred_element_type=jnp.float32))
            active_inner = low(jax.nn.silu(causal_filter(inner_raw, channel_params[:CONV], channel_params[CONV], segment)))
            active_state = low(jax.nn.silu(causal_filter(state_raw, state_filter[:CONV], state_filter[CONV], segment)))
            step_sizes = jax.nn.softplus(step_raw + head_params[0])
            mixed_heads = scan_states(active_inner.reshape(LENGTH, HEADS, HEAD_DIM), active_state[:, :D_STATE], active_state[:, D_STATE:], step_sizes, segment, -jnp.exp(head_params[1]), head_params[2])
            gated_out = mixed_heads.reshape(LENGTH, D_INNER) * jax.nn.silu(gate_raw)
            inverse = lax.rsqrt(lax.optimization_barrier(jnp.mean(gated_out * gated_out, -1, keepdims=True)) + NORM_EPS)
            normed_out = low(gated_out * inverse * channel_params[CONV + 1])
            return seq_rows + jnp.dot(normed_out, outer_weight.T, precision=HIGHEST, preferred_element_type=jnp.float32)
        return lax.map(jax.checkpoint(one_sequence), (stream, segments))
    block_output, pullback = jax.vjp(forward, stream, inner_proj, step_proj, state_proj, outer_proj, channel_params, head_params, state_filter, input_gain)
    grads = pullback(cotangent)
    inner_new = adam_update(inner_proj, grads[1], inner_first, inner_second, MATRIX_RATE, MATRIX_DECAY)
    step_new = adam_update(step_proj, grads[2], step_first, step_second, MATRIX_RATE, MATRIX_DECAY)
    state_new = adam_update(state_proj, grads[3], state_first, state_second, MATRIX_RATE, MATRIX_DECAY)
    outer_new = adam_update(outer_proj, grads[4], outer_first, outer_second, MATRIX_RATE, MATRIX_DECAY)
    channel_new = adam_update(channel_params, grads[5], channel_first, channel_second, VECTOR_RATE, 0.0)
    head_new = adam_update(head_params, grads[6], head_first, head_second, VECTOR_RATE, 0.0)
    filter_new = adam_update(state_filter, grads[7], filter_first, filter_second, VECTOR_RATE, 0.0)
    gain_new = adam_update(input_gain, grads[8], gain_first, gain_second, VECTOR_RATE, 0.0)
    return (block_output, grads[0], inner_new[0], inner_new[1], inner_new[2], step_new[0], step_new[1], step_new[2], state_new[0], state_new[1], state_new[2], outer_new[0], outer_new[1], outer_new[2], channel_new[0], channel_new[1], channel_new[2], head_new[0], head_new[1], head_new[2], filter_new[0], filter_new[1], filter_new[2], gain_new[0], gain_new[1], gain_new[2])
```

```python
from functools import partial

import jax
import jax.numpy as jnp
from jax import lax
from jax.experimental import pallas as pl
from jax.experimental.pallas import tpu as pltpu
from jax.sharding import PartitionSpec as P

SPAN = 256
STEP = 10


NORM_EPS = 1e-05
BETA_ONE = 0.9
BETA_TWO = 0.999
ADAM_EPS = 1e-08
MATRIX_RATE = 0.1
VECTOR_RATE = 0.3
MATRIX_DECAY = 0.1
HIGHEST = lax.Precision.HIGHEST


def matmul(left, right):
    return jnp.dot(left, right, preferred_element_type=jnp.float32)


def contract_rows(left, right):
    return lax.dot_general(
        left, right, (((0,), (0,)), ((), ())), preferred_element_type=jnp.float32
    )


def contract_last(left, right):
    return lax.dot_general(
        left, right, (((left.ndim - 1,), (1,)), ((), ())), preferred_element_type=jnp.float32
    )


def causal_filter(values, filter_taps, filter_bias, segment):
    taps_count = filter_taps.shape[0]
    seq_len = values.shape[-2]
    filtered = filter_bias + filter_taps[taps_count - 1] * values
    for offset in range(1, taps_count):
        leading = [(0, 0)] * (values.ndim - 2)
        shifted = jnp.pad(values, leading + [(offset, 0), (0, 0)])[..., :seq_len, :]
        earlier = jnp.pad(segment, leading + [(offset, 0)], constant_values=-1)[..., :seq_len]
        same_doc = (earlier == segment).astype(values.dtype)
        filtered = filtered + filter_taps[taps_count - 1 - offset] * shifted * same_doc[..., None]
    return filtered


def exact_dot(left, right):
    return jnp.dot(left, right, precision=HIGHEST, preferred_element_type=jnp.float32)


def rows_dot(left, right, precision=None):
    return lax.dot_general(
        left,
        right,
        (((0,), (0,)), ((), ())),
        precision=precision,
        preferred_element_type=jnp.float32,
    )


def lanes_dot(left, right):
    return lax.dot_general(
        left, right, (((1,), (1,)), ((), ())), preferred_element_type=jnp.float32
    )


def two_parts(value):
    high = value.astype(jnp.bfloat16)
    return high, (value - high.astype(jnp.float32)).astype(jnp.bfloat16)


def softplus(value):
    return jnp.maximum(value, 0.0) + jnp.log(1.0 + jnp.exp(-jnp.abs(value)))


def block_terms(heads, width, step_ref, marks_ref, seg_ref, head_ref):
    span = step_ref.shape[1]
    pre = step_ref[0] + head_ref[0:1, :]
    dt = softplus(pre)
    rates = -jnp.exp(head_ref[1:2, :])
    row = lax.broadcasted_iota(jnp.int32, (span, span), 0)
    col = lax.broadcasted_iota(jnp.int32, (span, span), 1)
    lower = jnp.where(row >= col, 1.0, 0.0).astype(jnp.float32)
    upper = jnp.where(row <= col, 1.0, 0.0).astype(jnp.float32)
    eye = jnp.where(row == col, 1.0, 0.0).astype(jnp.float32)
    scaled = dt * rates
    lam = exact_dot(lower, scaled)
    lam_row = rows_dot(scaled, upper, HIGHEST)
    dt_row = rows_dot(dt, eye, HIGHEST)
    marks = marks_ref[0]
    mask = (marks[:, 0:1] == seg_ref[0, 0]) & (row >= col)
    carried = marks[:, 1:2] * jnp.exp(lam)
    tail = marks[:, 2:3] * jnp.exp(lam[span - 1 : span, :] - lam) * dt
    lane = lax.broadcasted_iota(jnp.int32, (heads, heads * width), 1) // width
    head = lax.broadcasted_iota(jnp.int32, (heads, heads * width), 0)
    spread = jnp.where(lane == head, 1.0, 0.0).astype(jnp.float32)
    return pre, dt, rates, lam, lam_row, dt_row, mask, carried, tail, spread, upper


def decay_weights(lam, lam_row, dt_row, mask, h):
    gaps = jnp.where(mask, lam[:, h : h + 1] - lam_row[h : h + 1, :], -1e30)
    return jnp.exp(gaps) * dt_row[h : h + 1, :]


def scan_kernel(
    heads, width, x_ref, bc_ref, step_ref, marks_ref, seg_ref, head_ref, y_ref, save_ref, state
):
    n = bc_ref.shape[2] // 2

    @pl.when(pl.program_id(1) == 0)
    def _():
        state[...] = jnp.zeros_like(state)

    pre, dt, rates, lam, lam_row, dt_row, mask, carried, tail, spread, upper = block_terms(
        heads, width, step_ref, marks_ref, seg_ref, head_ref
    )
    b = bc_ref[0, :, :n]
    c = bc_ref[0, :, n:]
    scores = lanes_dot(c, b)
    old = state[...]
    save_ref[0, 0] = old
    x = x_ref[0].astype(jnp.float32)
    skip = exact_dot(head_ref[2:3, :], spread)
    span = x.shape[0]
    old_high, old_low = two_parts(old)
    rest = (matmul(c, old_high) + matmul(c, old_low)) * exact_dot(carried, spread) + skip * x
    pair = 2 * width
    side = lax.broadcasted_iota(jnp.int32, (span, pair), 1) < width
    for p in range(heads // 2):
        at = slice(p * pair, (p + 1) * pair)
        xp = x[:, at]
        left = jnp.where(side, xp, 0.0).astype(jnp.bfloat16)
        right = jnp.where(side, 0.0, xp).astype(jnp.bfloat16)
        high0, low0 = two_parts(decay_weights(lam, lam_row, dt_row, mask, 2 * p) * scores)
        high1, low1 = two_parts(decay_weights(lam, lam_row, dt_row, mask, 2 * p + 1) * scores)
        y_ref[0, :, at] = (
            (matmul(high0, left) + matmul(low0, left))
            + (matmul(high1, right) + matmul(low1, right))
            + rest[:, at]
        )
    kept = exact_dot(carried[span - 1 : span, :], spread)
    tail_high, tail_low = two_parts(x * exact_dot(tail, spread))
    state[...] = old * kept + (rows_dot(b, tail_high) + rows_dot(b, tail_low))


def back_kernel(
    heads,
    width,
    x_ref,
    bc_ref,
    step_ref,
    marks_ref,
    seg_ref,
    head_ref,
    y_ref,
    dy_ref,
    save_ref,
    dx_ref,
    dbc_ref,
    dstep_ref,
    skip_ref,
    small_ref,
    grad,
):
    n = bc_ref.shape[2] // 2

    @pl.when(pl.program_id(1) == 0)
    def _():
        grad[...] = jnp.zeros_like(grad)
        skip_ref[...] = jnp.zeros_like(skip_ref)
        small_ref[...] = jnp.zeros_like(small_ref)

    pre, dt, rates, lam, lam_row, dt_row, mask, carried, tail, spread, upper = block_terms(
        heads, width, step_ref, marks_ref, seg_ref, head_ref
    )
    b = bc_ref[0, :, :n]
    c = bc_ref[0, :, n:]
    scores = lanes_dot(c, b)
    x = x_ref[0].astype(jnp.float32)
    dy = dy_ref[0]
    skip = exact_dot(head_ref[2:3, :], spread)
    span = x.shape[0]
    old = save_ref[0, 0]
    later = grad[...]
    later_high, later_low = two_parts(later)
    tail_wide = exact_dot(tail, spread)
    carried_wide = exact_dot(carried, spread)
    tail_x = tail_wide * x
    carried_high, carried_low = two_parts(carried_wide * dy)
    from_state = matmul(b, later_high) + matmul(b, later_low)
    pair = 2 * width
    side = lax.broadcasted_iota(jnp.int32, (span, pair), 1) < width
    total = jnp.zeros((span, span), jnp.float32)
    pulled = []
    for p in range(heads // 2):
        at = slice(p * pair, (p + 1) * pair)
        dyp = dy[:, at]
        xp = x_ref[0, :, at]
        left = jnp.concatenate(two_parts(jnp.where(side, dyp, 0.0)), 1)
        right = jnp.concatenate(two_parts(jnp.where(side, 0.0, dyp)), 1)
        twice = jnp.concatenate([xp, xp], 1)
        d0 = decay_weights(lam, lam_row, dt_row, mask, 2 * p)
        d1 = decay_weights(lam, lam_row, dt_row, mask, 2 * p + 1)
        total = total + d0 * lanes_dot(left, twice) + d1 * lanes_dot(right, twice)
        high0, low0 = two_parts(d0 * scores)
        high1, low1 = two_parts(d1 * scores)
        both = (rows_dot(high0, left) + rows_dot(low0, left)) + (
            rows_dot(high1, right) + rows_dot(low1, right)
        )
        pulled.append(both[:, :pair] + both[:, pair:])
    inner = jnp.concatenate(pulled, 1)
    dx_ref[0] = inner + tail_wide * from_state + skip * dy
    total = total.astype(jnp.bfloat16)
    dbc_ref[0, :, :n] = rows_dot(total, c) + lanes_dot(tail_x.astype(jnp.bfloat16), later_high)
    dbc_ref[0, :, n:] = jnp.dot(total, b, preferred_element_type=jnp.float32) + lanes_dot(
        carried_high, old.astype(jnp.bfloat16)
    )
    gather = spread.T
    tail_part = exact_dot(tail_x * from_state, gather)
    columns = exact_dot(inner * x, gather) + tail_part
    rows = exact_dot(dy * (y_ref[0] - skip * x), gather)
    kept = carried[span - 1 : span, :]
    kept_wide = exact_dot(kept, spread)
    across = exact_dot(jnp.sum(later * old, axis=0, keepdims=True) * kept_wide, gather)
    end = across + jnp.sum(tail_part, axis=0, keepdims=True)
    lam_grad = exact_dot(upper, rows - columns) + end
    dt_grad = lam_grad * rates + columns / jnp.maximum(dt, 1e-30)
    dstep = dt_grad / (1.0 + jnp.exp(-pre))
    dstep_ref[0] = dstep
    skip_ref[0, 0:1, :] += jnp.sum(x * dy, axis=0, keepdims=True)
    small_ref[0, 0:1, :] += jnp.sum(dstep, axis=0, keepdims=True)
    small_ref[0, 1:2, :] += jnp.sum(dt * lam_grad, axis=0, keepdims=True) * rates
    grad[...] = later * kept_wide + (rows_dot(c, carried_high) + rows_dot(c, carried_low))


def scan_specs(blocks, back, heads, inner, states):
    def place(i):
        return blocks - 1 - i if back else i

    return [
        pl.BlockSpec((1, SPAN, inner), lambda s, i: (s, place(i), 0)),
        pl.BlockSpec((1, SPAN, states), lambda s, i: (s, place(i), 0)),
        pl.BlockSpec((1, SPAN, heads), lambda s, i: (s, place(i), 0)),
        pl.BlockSpec((1, SPAN, 8), lambda s, i: (s, place(i), 0)),
        pl.BlockSpec((1, 1, 1, SPAN), lambda s, i: (s, place(i), 0, 0)),
        pl.BlockSpec((3, heads), lambda s, i: (0, 0)),
    ], pl.BlockSpec((1, 1, states // 2, inner), lambda s, i: (s, place(i), 0, 0))


PARAMS = pltpu.CompilerParams(
    vmem_limit_bytes=48 * 1024 * 1024, dimension_semantics=("arbitrary", "arbitrary")
)


def scan_forward(x, bc, step_raw, marks, seg_rows, head_vec):
    count, length, inner = x.shape
    heads, states, blocks = head_vec.shape[1], bc.shape[2], x.shape[1] // SPAN
    specs, save = scan_specs(blocks, False, heads, inner, states)
    return pl.pallas_call(
        partial(scan_kernel, heads, inner // heads),
        grid=(count, blocks),
        in_specs=specs,
        out_specs=[specs[0], save],
        out_shape=[
            jax.ShapeDtypeStruct((count, length, inner), jnp.float32),
            jax.ShapeDtypeStruct((count, blocks, states // 2, inner), jnp.float32),
        ],
        scratch_shapes=[pltpu.VMEM((states // 2, inner), jnp.float32)],
        compiler_params=PARAMS,
        name="scan_forward",
    )(x, bc, step_raw, marks, seg_rows, head_vec)


def scan_backward(x, bc, step_raw, marks, seg_rows, head_vec, y, dy, saved):
    count, length, inner = x.shape
    heads, states, blocks = head_vec.shape[1], bc.shape[2], x.shape[1] // SPAN
    specs, save = scan_specs(blocks, True, heads, inner, states)
    return pl.pallas_call(
        partial(back_kernel, heads, inner // heads),
        grid=(count, blocks),
        in_specs=specs + [specs[0], specs[0], save],
        out_specs=[
            specs[0],
            specs[1],
            specs[2],
            pl.BlockSpec((1, 8, inner), lambda s, i: (s, 0, 0)),
            pl.BlockSpec((1, 8, heads), lambda s, i: (s, 0, 0)),
        ],
        out_shape=[
            jax.ShapeDtypeStruct((count, length, inner), jnp.float32),
            jax.ShapeDtypeStruct((count, length, states), jnp.float32),
            jax.ShapeDtypeStruct((count, length, heads), jnp.float32),
            jax.ShapeDtypeStruct((count, 8, inner), jnp.float32),
            jax.ShapeDtypeStruct((count, 8, heads), jnp.float32),
        ],
        scratch_shapes=[pltpu.VMEM((states // 2, inner), jnp.float32)],
        compiler_params=PARAMS,
        name="scan_backward",
    )(x, bc, step_raw, marks, seg_rows, head_vec, y, dy, saved)


def segment_marks(segment):
    count, length = segment.shape
    blocks = length // SPAN
    by_block = segment.reshape(count, blocks, SPAN)
    ends = by_block[:, :, SPAN - 1 :]
    before = jnp.pad(ends, ((0, 0), (1, 0), (0, 0)), constant_values=-1)[:, :blocks]
    columns = [by_block, by_block == before, by_block == ends]
    stacked = jnp.stack([v.astype(jnp.float32) for v in columns], -1)
    marks = jnp.pad(stacked, ((0, 0), (0, 0), (0, 0), (0, 5))).reshape(count, length, 8)
    return marks, by_block[:, :, None, :].astype(jnp.float32)


def filter_parts(segment, inner_raw, state_raw, channel_taps, state_taps):
    taps_count = state_taps.shape[0] - 1
    active_inner = jax.nn.silu(
        causal_filter(inner_raw, channel_taps[:taps_count], channel_taps[taps_count], segment)
    )
    active_state = jax.nn.silu(
        causal_filter(state_raw, state_taps[:taps_count], state_taps[taps_count], segment)
    )
    return (active_inner, active_state)


def adam_update(weight, gradient, moment_one, moment_two, step_rate, decay_rate):
    first_new = BETA_ONE * moment_one + (1.0 - BETA_ONE) * gradient
    second_new = BETA_TWO * moment_two + (1.0 - BETA_TWO) * gradient * gradient
    first_hat = first_new / (1.0 - BETA_ONE**STEP)
    second_hat = second_new / (1.0 - BETA_TWO**STEP)
    weight_new = weight - step_rate * (
        first_hat / (jnp.sqrt(second_hat) + ADAM_EPS) + decay_rate * weight
    )
    return (first_new, second_new, weight_new)


def shards(
    block_input,
    output_grad,
    segments,
    inner_proj,
    inner_first,
    inner_second,
    step_proj,
    step_first,
    step_second,
    state_proj,
    state_first,
    state_second,
    outer_proj,
    outer_first,
    outer_second,
    channel_params,
    channel_first,
    channel_second,
    head_params,
    head_first,
    head_second,
    state_filter,
    filter_first,
    filter_second,
    input_gain,
    gain_first,
    gain_second,
):
    sequence_count, quarter, model_width = block_input.shape
    tensor_size = lax.axis_size("tensor")
    tensor_rank = lax.axis_index("tensor")
    taps_count = state_filter.shape[0] - 1
    local_inner = inner_proj.shape[2]
    heads_here = step_proj.shape[1]
    state_cols = state_proj.shape[1]
    all_cols = lax.all_gather(
        jnp.concatenate(
            [
                inner_proj.reshape(-1, 2 * local_inner),
                state_proj,
                outer_proj,
                step_proj,
            ],
            1,
        ).astype(jnp.bfloat16),
        "dp",
        axis=0,
        tiled=True,
    )
    cut = 2 * local_inner
    inner_matrix = all_cols[:, :cut]
    state_weight = all_cols[:, cut : cut + state_cols]
    outer_weight = all_cols[:, cut + state_cols : cut + state_cols + local_inner]
    step_weight = all_cols[:, cut + state_cols + local_inner :]
    stream = block_input.astype(jnp.float32)
    row_scale = lax.rsqrt(jnp.mean(stream * stream, -1, keepdims=True) + NORM_EPS)
    unit_rows = stream * row_scale
    normed = (unit_rows * input_gain).astype(jnp.bfloat16)
    seq_rows, segment = (
        lax.all_gather(normed, "tensor", axis=1, tiled=True),
        lax.all_gather(segments, "tensor", axis=1, tiled=True),
    )
    length = seq_rows.shape[1]
    row_count = sequence_count * length
    flat_rows = seq_rows.reshape(row_count, model_width)
    mixed_cols = matmul(flat_rows, inner_matrix)
    gate_raw = mixed_cols[:, :local_inner].reshape(sequence_count, length, local_inner)
    inner_raw = mixed_cols[:, local_inner:].reshape(sequence_count, length, local_inner)
    step_raw = matmul(flat_rows, step_weight).reshape(sequence_count, length, heads_here)
    state_raw = matmul(flat_rows, state_weight).reshape(sequence_count, length, state_cols)
    (active_inner, active_state), filter_back = jax.vjp(
        partial(filter_parts, segment),
        inner_raw,
        state_raw,
        channel_params[: taps_count + 1],
        state_filter,
    )
    low_inner = lax.optimization_barrier(active_inner.astype(jnp.bfloat16))
    low_state = lax.optimization_barrier(active_state.astype(jnp.bfloat16))
    marks, seg_rows = segment_marks(segment)
    mixed, saved = scan_forward(low_inner, low_state, step_raw, marks, seg_rows, head_params)
    gate_open = jax.nn.sigmoid(gate_raw)
    gate_silu = gate_raw * gate_open
    gated_out = mixed * gate_silu
    squares = lax.psum(jnp.sum(gated_out * gated_out, -1), "tensor")
    inverse = lax.rsqrt(squares / (local_inner * tensor_size) + NORM_EPS)[..., None]
    gate_gain = channel_params[taps_count + 1]
    normed_out = (gated_out * inverse * gate_gain).astype(jnp.bfloat16)
    summed_parts = contract_last(normed_out.reshape(row_count, local_inner), outer_weight).reshape(
        sequence_count, length, model_width
    )
    own_out = lax.psum_scatter(
        summed_parts.astype(jnp.bfloat16), "tensor", scatter_dimension=1, tiled=True
    ).astype(jnp.float32)
    back_rows = lax.all_gather(output_grad, "tensor", axis=1, tiled=True).reshape(
        row_count, model_width
    )
    outer_grad = contract_rows(back_rows, normed_out.reshape(row_count, local_inner))
    outer_sum = lax.psum_scatter(outer_grad, "dp", scatter_dimension=0, tiled=True)
    normed_grad = matmul(back_rows, outer_weight).reshape(sequence_count, length, local_inner)
    scaled_grad = normed_grad * gate_gain
    dot_sums = lax.psum(jnp.sum(scaled_grad * gated_out, -1), "tensor")[..., None]
    gated_grad = inverse * scaled_grad - gated_out * inverse**3 * dot_sums / (
        local_inner * tensor_size
    )
    gain_grad = jnp.sum(normed_grad * gated_out * inverse, axis=(0, 1))
    dy = gated_grad * gate_silu
    gate_back = gated_grad * mixed * (gate_open * (1.0 + gate_raw * (1.0 - gate_open)))
    inner_back, state_back, step_back, skip_sums, small_sums = scan_backward(
        low_inner, low_state, step_raw, marks, seg_rows, head_params, mixed, dy, saved
    )
    inner_back, own_out, outer_sum = lax.optimization_barrier((inner_back, own_out, outer_sum))
    block_output = stream + own_out
    head_grad = jnp.concatenate(
        [
            jnp.sum(small_sums[:, :2], 0),
            jnp.sum(skip_sums[:, 0].reshape(sequence_count, heads_here, -1), (0, 2))[None],
        ],
        0,
    )
    state_total = lax.psum(state_back.astype(jnp.bfloat16), "tensor").astype(jnp.float32)
    inner_pre, state_pre, taps_grad, filter_grad = filter_back((inner_back, state_total))
    both_low = jnp.concatenate([gate_back.astype(jnp.bfloat16), inner_pre.astype(jnp.bfloat16)], -1)
    step_low = step_back.astype(jnp.bfloat16)
    state_low = state_pre.astype(jnp.bfloat16)
    wide_low = jnp.concatenate([both_low, state_low, step_low], -1).reshape(row_count, -1)
    wide_grad = contract_rows(flat_rows, wide_low)
    wide_sum = lax.psum_scatter(wide_grad, "dp", scatter_dimension=0, tiled=True)
    inner_sum = wide_sum[:, :cut].reshape(-1, 2, local_inner)
    state_sum = wide_sum[:, cut : cut + state_cols]
    step_sum = wide_sum[:, cut + state_cols :]
    summed_grads = contract_last(
        both_low.reshape(row_count, 2 * local_inner), inner_matrix
    ) + contract_last(step_low.reshape(row_count, heads_here), step_weight)
    own_grad = lax.psum_scatter(
        summed_grads.reshape(sequence_count, length, model_width).astype(jnp.bfloat16),
        "tensor",
        scatter_dimension=1,
        tiled=True,
    ).astype(jnp.float32)
    own_state = lax.dynamic_slice_in_dim(state_low, tensor_rank * quarter, quarter, 1)
    own_grad = own_grad + contract_last(own_state, state_weight)
    scaled_in = own_grad * input_gain
    input_grad = output_grad.astype(jnp.float32) + row_scale * (
        scaled_in - unit_rows * jnp.mean(scaled_in * unit_rows, -1, keepdims=True)
    )
    input_gain_grad = jnp.sum(own_grad * unit_rows, axis=(0, 1))
    channel_grad = jnp.concatenate([taps_grad, gain_grad[None, :]], 0)
    wide_channel = lax.dynamic_update_slice(
        jnp.zeros((channel_grad.shape[0], local_inner * tensor_size), jnp.float32),
        channel_grad,
        (0, tensor_rank * local_inner),
    )
    wide_head = lax.dynamic_update_slice(
        jnp.zeros((head_grad.shape[0], heads_here * tensor_size), jnp.float32),
        head_grad,
        (0, tensor_rank * heads_here),
    )
    leader = (tensor_rank == 0).astype(jnp.float32)
    channel_all, head_all, filter_all, gain_all = lax.psum(
        (wide_channel, wide_head, filter_grad * leader, input_gain_grad), ("dp", "tensor")
    )
    channel_sum = lax.dynamic_slice_in_dim(channel_all, tensor_rank * local_inner, local_inner, 1)
    head_sum = lax.dynamic_slice_in_dim(head_all, tensor_rank * heads_here, heads_here, 1)
    inner_new = adam_update(
        inner_proj, inner_sum, inner_first, inner_second, MATRIX_RATE, MATRIX_DECAY
    )
    step_new = adam_update(step_proj, step_sum, step_first, step_second, MATRIX_RATE, MATRIX_DECAY)
    state_new = adam_update(
        state_proj, state_sum, state_first, state_second, MATRIX_RATE, MATRIX_DECAY
    )
    outer_new = adam_update(
        outer_proj, outer_sum, outer_first, outer_second, MATRIX_RATE, MATRIX_DECAY
    )
    channel_new = adam_update(
        channel_params, channel_sum, channel_first, channel_second, VECTOR_RATE, 0.0
    )
    head_new = adam_update(head_params, head_sum, head_first, head_second, VECTOR_RATE, 0.0)
    filter_new = adam_update(
        state_filter, filter_all, filter_first, filter_second, VECTOR_RATE, 0.0
    )
    gain_new = adam_update(input_gain, gain_all, gain_first, gain_second, VECTOR_RATE, 0.0)
    return (
        block_output,
        input_grad,
        inner_new[0],
        inner_new[1],
        inner_new[2],
        step_new[0],
        step_new[1],
        step_new[2],
        state_new[0],
        state_new[1],
        state_new[2],
        outer_new[0],
        outer_new[1],
        outer_new[2],
        channel_new[0],
        channel_new[1],
        channel_new[2],
        head_new[0],
        head_new[1],
        head_new[2],
        filter_new[0],
        filter_new[1],
        filter_new[2],
        gain_new[0],
        gain_new[1],
        gain_new[2],
    )


def solution(mesh):
    return jax.shard_map(
        shards,
        mesh=mesh,
        in_specs=(
            P("dp", "tensor", None),
            P("dp", "tensor", None),
            P("dp", "tensor"),
            P("dp", None, "tensor"),
            P("dp", None, "tensor"),
            P("dp", None, "tensor"),
            P("dp", "tensor"),
            P("dp", "tensor"),
            P("dp", "tensor"),
            P("dp", None),
            P("dp", None),
            P("dp", None),
            P("dp", "tensor"),
            P("dp", "tensor"),
            P("dp", "tensor"),
            P(None, "tensor"),
            P(None, "tensor"),
            P(None, "tensor"),
            P(None, "tensor"),
            P(None, "tensor"),
            P(None, "tensor"),
            P(),
            P(),
            P(),
            P(),
            P(),
            P(),
        ),
        out_specs=(
            P("dp", "tensor", None),
            P("dp", "tensor", None),
            P("dp", None, "tensor"),
            P("dp", None, "tensor"),
            P("dp", None, "tensor"),
            P("dp", "tensor"),
            P("dp", "tensor"),
            P("dp", "tensor"),
            P("dp", None),
            P("dp", None),
            P("dp", None),
            P("dp", "tensor"),
            P("dp", "tensor"),
            P("dp", "tensor"),
            P(None, "tensor"),
            P(None, "tensor"),
            P(None, "tensor"),
            P(None, "tensor"),
            P(None, "tensor"),
            P(None, "tensor"),
            P(),
            P(),
            P(),
            P(),
            P(),
            P(),
        ),
        check_vma=False,
    )
```
